1024 devices in a mesh: gx: 8 (over y), gy: 4 (over x), gz: 32 (over z, core).
Axes of the slice: x: 4, y: 8, z: 16, core: 2. Of those that a mesh axis runs over, the one named last changes fastest.
Arguments:
- tokens: bfloat16 [512, 10240], P('gy', ('gx', 'gz')), may hold values from -6 to 6
- w_up: bfloat16 [10240, 15872], P('gx', ('gz', 'gy')), may hold values from -0.0625 to 0.0625
- w_down: bfloat16 [15872, 10240], P(('gz', 'gy'), 'gx'), may hold values from -0.046875 to 0.046875
- out_grad: bfloat16 [512, 10240], P('gy', ('gx', 'gz')), may hold values from -6 to 6
Outputs:
- output: bfloat16 [512, 10240], P('gy', ('gx', 'gz'))
- grad_tokens: bfloat16 [512, 10240], P('gy', ('gx', 'gz'))
- grad_up: bfloat16 [10240, 15872], P('gx', ('gz', 'gy'))
- grad_down: bfloat16 [15872, 10240], P(('gz', 'gy'), 'gx')
The draws below stay inside these ranges and needn't reach their ends.
All inputs are finite; a program needn't handle non-finite values.
Results may differ from the reference program's by a relative error of at most 0.0049.
Values may be sent and summed in bfloat16 or wider, within the bound.
A program may use at most 32 MiB of HBM per device.

```python
import math
import jax
import jax.numpy as jnp
from jax import lax

D = 10240
FF = 15872
TOKENS = 512


def shard_levels(key, dims, pieces, least, high):
    factor_of = 1.0
    for axis_at, blocks in pieces:
        heights = jax.random.uniform(jax.random.fold_in(jax.random.fold_in(key, 6), axis_at), (blocks,), jnp.float32, least / len(pieces), high / len(pieces))
        factor_of = factor_of * jnp.repeat(jnp.exp(heights), dims[axis_at] // blocks).reshape((-1,) + (1,) * (len(dims) - 1 - axis_at))
    return factor_of


def gaussian(stream_key, shape, width, bound, shards=(), kind=jnp.bfloat16):
    values = jax.random.normal(stream_key, shape, jnp.float32) * width
    if len(shards) > 0:
        values = shard_levels(stream_key, shape, shards, -0.22, 0.18) * values
    return jnp.clip(values, min=-bound, max=bound).astype(kind)


def setup_inputs(seed: int = 0) -> dict:
    arg_keys = jax.random.split(jax.random.key(seed), 5)
    tokens = gaussian(arg_keys[0], (TOKENS, D), 1.0, 6.0, ((0, 4), (1, 256)))
    w_up = gaussian(arg_keys[1], (D, FF), D ** -0.5, 0.0625, ((0, 8), (1, 128)))
    w_down = gaussian(arg_keys[2], (FF, D), FF ** -0.5, 0.046875, ((0, 128), (1, 8)))
    out_grad = gaussian(arg_keys[3], (TOKENS, D), 1.0, 6.0, ((0, 4), (1, 256)))
    return {"tokens": tokens, "w_up": w_up, "w_down": w_down, "out_grad": out_grad}


def gelu_parts(pre):
    cdf = 0.5 * (1.0 + jax.scipy.special.erf(pre / math.sqrt(2.0)))
    dens = jnp.exp(-0.5 * pre * pre) / math.sqrt(2.0 * math.pi)
    return (pre * cdf, cdf + pre * dens)

def contract_first(left, right):
    return lax.dot_general(left, right, (((0,), (0,)), ((), ())), preferred_element_type=jnp.float32)

def contract_last(left, right):
    return lax.dot_general(left, right, (((1,), (1,)), ((), ())), preferred_element_type=jnp.float32)

def reference(tokens, w_up, w_down, out_grad):
    pre = jnp.dot(tokens, w_up, preferred_element_type=jnp.float32)
    value, slope = gelu_parts(pre)
    hidden = value.astype(jnp.bfloat16)
    output = jnp.dot(hidden, w_down, preferred_element_type=jnp.float32).astype(jnp.bfloat16)
    grad_hidden = contract_last(out_grad, w_down)
    grad_pre = (grad_hidden * slope).astype(jnp.bfloat16)
    grad_tokens = contract_last(grad_pre, w_up).astype(jnp.bfloat16)
    grad_up = contract_first(tokens, grad_pre).astype(jnp.bfloat16)
    grad_down = contract_first(hidden, out_grad).astype(jnp.bfloat16)
    return (output, grad_tokens, grad_up, grad_down)
```

```python
import functools
import math

import jax
import jax.numpy as jnp
from jax import lax
from jax.experimental import pallas as pl
from jax.experimental.pallas import tpu as pltpu
from jax.sharding import PartitionSpec as P

MESH = pl.DeviceIdType.MESH
BF16, F32 = jnp.bfloat16, jnp.float32
LANES = 128


def dot(left, right, dims=((1,), (0,))):
    return lax.dot_general(left, right, (dims, ((), ())), preferred_element_type=F32)


def kernel(sizes, *refs):
    nx, ny, nz, rows, half, fcols = sizes
    (tok, cot, w_up, w_dn, o_out, o_gt, o_gu, o_gd,
     tile, pair_in, own_f, pad_out, xt, w, wt, give_up, give_dn,
     part_f, part_b, got_b, share, other, ht,
     send_c, got_x, own_c, send_z, got_z, final, out_give, out_got,
     g_give_up, g_give_dn, g_got_up, g_got_dn,
     s_pair, r_pair, s_az, r_az, s_ax, r_ax, s_b, r_b, s_h, r_h, s_cx, r_cx, s_cz, r_cz) = refs
    y, x = lax.axis_index("gx"), lax.axis_index("gy")
    g = lax.axis_index("gz")
    z, c = lax.div(g, 2), lax.rem(g, 2)
    width = xt.shape[0]
    tokens = xt.shape[1]
    hid = ht.shape[0]
    hrows = hid // ny

    def dev(yy, xx, zz, cc):
        return (yy, xx, zz * 2 + cc)

    partner = dev(y, x, z, 1 - c)

    def at_x(k):
        return dev(y, lax.rem(x + k, nx), z, c)

    def at_y(k):
        return dev(lax.rem(y + k, ny), x, z, c)

    def at_z(k):
        return dev(y, x, lax.rem(z + k, nz), c)

    def remote(src, dst, ssem, rsem, device):
        return pltpu.make_async_remote_copy(
            src_ref=src, dst_ref=dst, send_sem=ssem, recv_sem=rsem, device_id=device, device_id_type=MESH)

    def loop(n, body):
        def step(i, carry):
            body(i)
            return carry
        lax.fori_loop(0, n, step, 0)

    def far_first(i):
        m = lax.div(i + 1, 2)
        return nz // 2 + m * (2 * lax.rem(i + 1, 2) - 1)

    def rblock(i):
        return pl.ds(pl.multiple_of(i * rows, 16), rows)

    def lblock(i):
        return pl.ds(pl.multiple_of(i * LANES, LANES), LANES)

    barrier = pltpu.get_barrier_semaphore()

    def hello(device):
        pl.semaphore_signal(barrier, inc=1, device_id=device, device_id_type=MESH)

    hello(partner)
    loop(nz - 1, lambda i: hello(at_z(i + 1)))
    loop(nx - 1, lambda i: hello(at_x(i + 1)))
    loop(ny - 1, lambda i: hello(at_y(i + 1)))

    first = c == 0
    tile[...] = jnp.zeros_like(tile)
    tile[0, :, :half] = jnp.where(first, tok[...], cot[...])
    tile[1, :, :half] = jnp.where(first, cot[...], tok[...])
    pl.semaphore_wait(barrier, 1 + (nz - 1) + (nx - 1) + (ny - 1))
    to_pair = remote(tile.at[1], pair_in, s_pair.at[0], r_pair.at[0], partner)
    to_pair.start()
    mine = tile[0].astype(F32).T[:half]
    own_f[pl.ds(pl.multiple_of(c * half, 8), half), :] = mine
    to_pair.wait_recv()
    theirs = pair_in[...].astype(F32).T[:half]
    own_f[pl.ds(pl.multiple_of((1 - c) * half, 8), half), :] = theirs
    xt[rblock(z), lblock(x)] = own_f[...].astype(BF16)

    def block(zz):
        return xt.at[rblock(zz), lblock(x)]

    def over_z(i):
        k = far_first(i)
        return remote(block(z), block(z), s_az.at[k], r_az.at[z], at_z(k))

    def over_x(k, zz):
        return remote(block(zz), block(zz), s_ax.at[k, zz], r_ax.at[k, zz], at_x(k))

    loop(nz - 1, lambda i: over_z(i).start())
    loop(nx - 1, lambda i: over_x(i + 1, z).start())

    @pl.when(first)
    def _():
        w[:, :LANES] = jnp.zeros((width, LANES), BF16)
        w[:, :fcols] = w_up[...]
        give_dn[...] = jnp.zeros_like(give_dn)
        give_dn[:fcols, :] = w_dn[...]
        remote(give_dn, wt.at[:LANES, :], s_pair.at[1], r_pair.at[1], partner).start()

    @pl.when(c == 1)
    def _():
        give_up[...] = jnp.zeros_like(give_up)
        give_up[:, :fcols] = w_up[...]
        remote(give_up, w.at[:, LANES:], s_pair.at[2], r_pair.at[2], partner).start()
        wt[LANES:, :] = jnp.zeros((LANES, width), BF16)
        wt[LANES:LANES + fcols, :] = w_dn[...]

    def hand_on(j):
        zz = nz - 1 - j

        @pl.when(zz != z)
        def _():
            remote(block(zz), block(zz), s_az.at[0], r_az.at[zz], at_x(1)).wait_recv()
            for k in range(1, nx):
                over_x(k, zz).start()

    @pl.when(first)
    def _():
        remote(give_up, w.at[:, LANES:], s_pair.at[1], r_pair.at[2], partner).wait_recv()

        def turn(i):
            tall = pl.ds(pl.multiple_of(i * LANES, LANES), LANES)
            wt[:, tall] = w[tall, :].T
        loop(width // LANES, turn)

    @pl.when(c == 1)
    def _():
        remote(give_dn, wt.at[:LANES, :], s_pair.at[2], r_pair.at[1], partner).wait_recv()

        def turn(i):
            tall = pl.ds(pl.multiple_of(i * LANES, LANES), LANES)
            w[tall, :] = wt[:, tall].T
        loop(width // LANES, turn)

    loop(nz, hand_on)

    def arrived(i):
        for k in range(1, nx):
            landing = xt.at[rblock(i), lblock(lax.rem(x + nx - k, nx))]
            remote(landing, landing, s_ax.at[k, i], r_ax.at[k, i], at_x(1)).wait_recv()
    loop(nz, arrived)

    def first_product(i):
        cols = pl.ds(pl.multiple_of(i * LANES, LANES), LANES)
        p = dot(wt[...], xt[:, cols])
        part_f[:, cols] = p
        part_b[:, cols] = p.astype(BF16)
    loop(tokens // LANES, first_product)

    def hblock(i):
        return pl.ds(pl.multiple_of(i * hrows, 16), hrows)

    def share_of(k):
        return remote(part_b.at[hblock(lax.rem(y + k, ny)), :], got_b.at[k], s_b.at[k], r_b.at[k], at_y(k))

    y_order = sorted(range(1, ny), key=lambda k: -min(k, ny - k))
    for k in y_order:
        share_of(k).start()
    total = part_f[hblock(y), :]
    for k in reversed(y_order):
        share_of(k).wait_recv()
        total = total + got_b[k].astype(F32)
    share[...] = total
    swap = remote(share, other, s_pair.at[3], r_pair.at[3], partner)
    swap.start()
    swap.wait_recv()
    pre = jnp.where(first, total, other[...])
    cdf = 0.5 * (1.0 + lax.erf(pre * (1.0 / math.sqrt(2.0))))
    dens = jnp.exp(-0.5 * pre * pre) * (1.0 / math.sqrt(2.0 * math.pi))
    made = jnp.where(first, other[...] * (cdf + pre * dens), pre * cdf)
    ht[hblock(y), :] = made.astype(BF16)

    def spread(k):
        return remote(ht.at[hblock(y), :], ht.at[hblock(y), :], s_h.at[k], r_h.at[k], at_y(k))

    for k in y_order:
        spread(k).start()
    for k in reversed(y_order):
        landing = ht.at[hblock(lax.rem(y + ny - k, ny)), :]
        remote(landing, landing, s_h.at[k], r_h.at[k], at_y(1)).wait_recv()

    def to_x(k, d):
        return remote(send_c.at[rblock(d), lblock(lax.rem(x + k, nx))], got_x.at[k, rblock(d), :],
                      s_cx.at[k, d], r_cx.at[k, d], at_x(k))

    def second_product(i):
        d = lax.rem(z + far_first(i), nz)
        p = dot(w[rblock(d), :], ht[...])
        own_c[rblock(d), :] = jnp.zeros((rows, LANES), F32)
        send_c[rblock(d), :] = p.astype(BF16)
        for k in range(nx):
            @pl.when(x == k)
            def _(k=k):
                own_c[rblock(d), :] = p[:, k * LANES:(k + 1) * LANES]
        for k in (2, 1, 3):
            to_x(k, d).start()
    loop(nz, second_product)

    step_rows = 2 * LANES

    @pl.when(first)
    def _():
        def grad(i):
            tall = pl.ds(pl.multiple_of(i * step_rows, step_rows), step_rows)
            p = dot(xt[tall, :], ht[...], ((1,), (1,))).astype(BF16)
            o_gu[tall, :] = p[:, :fcols]
            g_give_up[tall, :] = p[:, LANES:]
        loop(width // step_rows, grad)
        remote(g_give_up, g_got_up, s_pair.at[4], r_pair.at[4], partner).start()

    @pl.when(c == 1)
    def _():
        def grad(i):
            tall = pl.ds(pl.multiple_of(i * step_rows, step_rows), step_rows)
            p = dot(ht[...], xt[tall, :], ((1,), (1,))).astype(BF16)
            g_give_dn[:, tall] = p[:LANES, :]
            o_gd[:, tall] = p[LANES:LANES + fcols, :]
        loop(width // step_rows, grad)
        remote(g_give_dn, g_got_dn, s_pair.at[5], r_pair.at[5], partner).start()

    def to_z(k):
        d = lax.rem(z + k, nz)
        return remote(send_z.at[rblock(d), :], got_z.at[z], s_cz.at[k], r_cz.at[z], at_z(k))

    def add_x(d):
        total = own_c[rblock(d), :]
        for k in range(1, nx):
            to_x(k, d).wait_recv()
            total = total + got_x[k, rblock(d), :].astype(F32)
        return total

    def pass_on(i):
        k = far_first(i)
        d = lax.rem(z + k, nz)
        send_z[rblock(d), :] = add_x(d).astype(BF16)
        to_z(k).start()
    loop(nz - 1, pass_on)
    final[:rows, :] = add_x(z)

    def collect(i):
        s = lax.rem(z + far_first(nz - 2 - i), nz)
        remote(got_z.at[s], got_z.at[s], s_cz.at[1], r_cz.at[s], at_z(1)).wait_recv()
        final[:rows, :] += got_z[s].astype(F32)
    loop(nz - 1, collect)

    pad_out[...] = jnp.zeros_like(pad_out)
    pad_out[0, :half, :] = final[pl.ds(pl.multiple_of(c * half, 8), half), :]
    pad_out[1, :half, :] = final[pl.ds(pl.multiple_of((1 - c) * half, 8), half), :]
    out_give[...] = pad_out[1].T.astype(BF16)
    back = remote(out_give, out_got, s_pair.at[6], r_pair.at[6], partner)
    back.start()
    kept = pad_out[0].T.astype(BF16)[:, :half]

    @pl.when(first)
    def _():
        remote(g_give_dn, g_got_dn, s_pair.at[4], r_pair.at[5], partner).wait_recv()
        o_gd[...] = g_got_dn[:fcols, :]
        o_gt[...] = kept
        back.wait_recv()
        o_out[...] = out_got[:, :half]
        remote(give_dn, wt.at[:LANES, :], s_pair.at[1], r_pair.at[1], partner).wait_send()
        remote(g_give_up, g_got_up, s_pair.at[4], r_pair.at[4], partner).wait_send()

    @pl.when(c == 1)
    def _():
        remote(g_give_up, g_got_up, s_pair.at[5], r_pair.at[4], partner).wait_recv()
        o_gu[...] = g_got_up[:, :fcols]
        o_out[...] = kept
        back.wait_recv()
        o_gt[...] = out_got[:, :half]
        remote(give_up, w.at[:, LANES:], s_pair.at[2], r_pair.at[2], partner).wait_send()
        remote(g_give_dn, g_got_dn, s_pair.at[5], r_pair.at[5], partner).wait_send()

    to_pair.wait_send()
    swap.wait_send()
    back.wait_send()
    for k in y_order:
        share_of(k).wait_send()
        spread(k).wait_send()
    loop(nz - 1, lambda i: over_z(i).wait_send())
    loop(nz - 1, lambda i: to_z(far_first(i)).wait_send())

    def sent(i):
        for k in range(1, nx):
            over_x(k, i).wait_send()
            to_x(k, i).wait_send()
    loop(nz, sent)


def local(shape, tokens, w_up, w_down, out_grad):
    nx, ny, nz = shape["gy"], shape["gx"], shape["gz"] // 2
    half = tokens.shape[1]
    rows = 2 * half
    width, fcols = w_up.shape
    count = tokens.shape[0] * nx
    hid = 2 * LANES
    vmem, dma = pltpu.VMEM, pltpu.SemaphoreType.DMA
    scratch = [
        vmem((2, LANES, LANES), BF16), vmem((LANES, LANES), BF16), vmem((rows, LANES), F32),
        vmem((2, LANES, LANES), F32),
        vmem((width, count), BF16), vmem((width, hid), BF16), vmem((hid, width), BF16),
        vmem((width, LANES), BF16), vmem((LANES, width), BF16),
        vmem((hid, count), F32), vmem((hid, count), BF16), vmem((ny, hid // ny, count), BF16),
        vmem((hid // ny, count), F32), vmem((hid // ny, count), F32), vmem((hid, count), BF16),
        vmem((width, count), BF16), vmem((nx, width, LANES), BF16), vmem((width, LANES), F32),
        vmem((width, LANES), BF16), vmem((nz, rows, LANES), BF16), vmem((rows, LANES), F32),
        vmem((LANES, LANES), BF16), vmem((LANES, LANES), BF16),
        vmem((width, LANES), BF16), vmem((LANES, width), BF16),
        vmem((width, LANES), BF16), vmem((LANES, width), BF16),
        dma((7,)), dma((7,)), dma((nz,)), dma((nz,)), dma((nx, nz)), dma((nx, nz)),
        dma((ny,)), dma((ny,)), dma((ny,)), dma((ny,)),
        dma((nx, nz)), dma((nx, nz)), dma((nz,)), dma((nz,)),
    ]
    whole = pl.BlockSpec(memory_space=pltpu.VMEM)
    return pl.pallas_call(
        functools.partial(kernel, (nx, ny, nz, rows, half, fcols)),
        out_shape=(
            jax.ShapeDtypeStruct(tokens.shape, BF16), jax.ShapeDtypeStruct(tokens.shape, BF16),
            jax.ShapeDtypeStruct(w_up.shape, BF16), jax.ShapeDtypeStruct(w_down.shape, BF16)),
        in_specs=[whole] * 4,
        out_specs=(whole,) * 4,
        scratch_shapes=scratch,
        compiler_params=pltpu.CompilerParams(
            collective_id=0, has_side_effects=True, vmem_limit_bytes=48 * 1024 * 1024),
    )(tokens, out_grad, w_up, w_down)


def solution(mesh):
    tokens, up, down = P("gy", ("gx", "gz")), P("gx", ("gz", "gy")), P(("gz", "gy"), "gx")
    return jax.shard_map(
        functools.partial(local, dict(mesh.shape)),
        mesh=mesh,
        in_specs=(tokens, up, down, tokens),
        out_specs=(tokens, tokens, up, down),
        check_vma=False,
    )
```

```python
import functools
import math

import jax
import jax.numpy as jnp
from jax import lax
from jax.experimental import pallas as pl
from jax.experimental.pallas import tpu as pltpu
from jax.sharding import PartitionSpec as P

MESH = pl.DeviceIdType.MESH
BF16, F32 = jnp.bfloat16, jnp.float32
LANES = 128


def dot(left, right, dims=((1,), (0,))):
    return lax.dot_general(left, right, (dims, ((), ())), preferred_element_type=F32)


def kernel(sizes, *refs):
    nx, ny, nz, rows, half, fcols = sizes
    (tok, cot, w_up, w_dn, o_out, o_gt, o_gu, o_gd,
     give, pair_in, own_f, xt, w, wt, give_up, give_dn,
     part_f, part_b, got_b, share, other, ht,
     send_c, got_x, own_c, send_z, got_z, final, out_give, out_got,
     g_give_up, g_give_dn, g_got_up, g_got_dn,
     s_pair, r_pair, s_far, r_far, s_near, r_near, s_ax, r_ax, s_swap, r_swap, s_b, r_b, s_h, r_h, s_cx, r_cx, s_cz, r_cz) = refs
    y, x = lax.axis_index("gx"), lax.axis_index("gy")
    g = lax.axis_index("gz")
    z, c = lax.div(g, 2), lax.rem(g, 2)
    width = xt.shape[0]
    tokens = xt.shape[1]
    hid = ht.shape[0]
    hrows = hid // ny

    def dev(yy, xx, zz, cc):
        return (yy, xx, zz * 2 + cc)

    partner = dev(y, x, z, 1 - c)

    def at_x(k):
        return dev(y, lax.rem(x + k, nx), z, c)

    def at_y(k):
        return dev(lax.rem(y + k, ny), x, z, c)

    def at_z(k):
        return dev(y, x, lax.rem(z + k, nz), c)

    def remote(src, dst, ssem, rsem, device):
        return pltpu.make_async_remote_copy(
            src_ref=src, dst_ref=dst, send_sem=ssem, recv_sem=rsem, device_id=device, device_id_type=MESH)

    def loop(n, body):
        def step(i, carry):
            body(i)
            return carry
        lax.fori_loop(0, n, step, 0)

    def far_first(i):
        m = lax.div(i + 1, 2)
        return nz // 2 + m * (2 * lax.rem(i + 1, 2) - 1)

    def rblock(i):
        return pl.ds(pl.multiple_of(i * rows, 16), rows)

    def lblock(i):
        return pl.ds(pl.multiple_of(i * LANES, LANES), LANES)

    barrier = pltpu.get_barrier_semaphore()

    def hello(device):
        pl.semaphore_signal(barrier, inc=1, device_id=device, device_id_type=MESH)

    loop(nz - 1, lambda i: hello(at_z(far_first(i))))
    for k in range(1, ny):
        hello(at_y(k))
    for k in range(1, nx):
        hello(at_x(k))
    hello(partner)

    first = c == 0
    give[...] = jnp.zeros_like(give)
    give[:half, :] = jnp.where(first, cot[...], tok[...])
    own_f[pl.ds(pl.multiple_of(c * half, 8), half), :] = jnp.where(first, tok[...], cot[...]).astype(F32)
    give_dn[...] = jnp.zeros_like(give_dn)
    give_up[...] = jnp.zeros_like(give_up)
    give_dn[:fcols, :] = w_dn[...]
    give_up[:, :fcols] = w_up[...]

    order = (0, 2, 1, 3)
    place = {k: at for at, k in enumerate(order)}
    to_pair = remote(give, pair_in, s_pair.at[0], r_pair.at[0], partner)
    far = (nz // 2, nz // 4, 3 * nz // 4, 0)
    near = (2 + (nz - 4) * c, 1 + (nz - 2) * c, nz - 1 - (nz - 2) * c)

    def back_by(k):
        return lax.rem(z + 2 * nz - k, nz)

    def block(zz, at=0):
        return xt.at[rblock(zz), at * LANES:(at + 1) * LANES]

    def over_far(q):
        return remote(block(z), block(z), s_far.at[q], r_far.at[q], at_z(far[q]))

    def over_near(q, j):
        zz = back_by(far[q])
        return remote(block(zz), block(zz), s_near.at[q, j], r_near.at[q, j], at_z(near[j]))

    def over_x(k, zz):
        return remote(block(zz), block(zz, place[(nx - k) % nx]), s_ax.at[k, zz], r_ax.at[k, zz], at_x(k))

    def send_over_x(zz):
        for k in (2, 1, 3):
            over_x(k, zz).start()

    pl.semaphore_wait(barrier, 1 + (nz - 1) + (nx - 1) + (ny - 1))
    to_pair.start()
    to_pair.wait_recv()
    own_f[pl.ds(pl.multiple_of((1 - c) * half, 8), half), :] = pair_in[:half, :].astype(F32)
    xt[rblock(z), :LANES] = own_f[...].astype(BF16)
    for q in range(3):
        over_far(q).start()
    for j in range(3):
        over_near(3, j).start()
    send_over_x(z)

    @pl.when(first)
    def _():
        remote(give_dn, wt.at[:LANES, :], s_pair.at[1], r_pair.at[1], partner).start()

    @pl.when(c == 1)
    def _():
        remote(give_up, w.at[:, LANES:], s_pair.at[2], r_pair.at[2], partner).start()

    def take_near(q, j):
        zz = back_by(far[q] + near[j])
        remote(block(zz), block(zz), s_near.at[q, j], r_near.at[q, j], at_z(1)).wait_recv()
        send_over_x(zz)

    @pl.when(first)
    def _():
        w[:, :LANES] = give_up[...]
        remote(give_up, w.at[:, LANES:], s_pair.at[1], r_pair.at[2], partner).wait_recv()

        def turn(i):
            tall = pl.ds(pl.multiple_of(i * LANES, LANES), LANES)
            wt[:, tall] = w[tall, :].T
        loop(width // LANES, turn)

    @pl.when(c == 1)
    def _():
        wt[LANES:, :] = give_dn[...]
        remote(give_dn, wt.at[:LANES, :], s_pair.at[2], r_pair.at[1], partner).wait_recv()

        def turn(i):
            tall = pl.ds(pl.multiple_of(i * LANES, LANES), LANES)
            w[tall, :] = wt[:, tall].T
        loop(width // LANES, turn)

    take_near(3, 1)
    take_near(3, 2)
    for q in (1, 2, 0):
        zz = back_by(far[q])
        remote(block(zz), block(zz), s_far.at[q], r_far.at[q], at_z(1)).wait_recv()
        for j in range(3):
            over_near(q, j).start()
        send_over_x(zz)
    take_near(3, 0)
    for q in (1, 2, 0):
        for j in (1, 2, 0):
            take_near(q, j)

    chunks = ((0, 1), (1, 2), (3, 1))

    def lanes(ch):
        return pl.ds(chunks[ch][0] * LANES, chunks[ch][1] * LANES)

    def hblock(i):
        return pl.ds(pl.multiple_of(i * hrows, 16), hrows)

    y_order = sorted(range(1, ny), key=lambda k: -min(k, ny - k))

    def share_of(ch, k):
        return remote(part_b.at[hblock(lax.rem(y + k, ny)), lanes(ch)], got_b.at[k, :, lanes(ch)],
                      s_b.at[ch, k], r_b.at[ch, k], at_y(k))

    def swap(ch):
        return remote(share.at[:, lanes(ch)], other.at[:, lanes(ch)], s_swap.at[ch], r_swap.at[ch], partner)

    def spread(ch, k):
        rows_of = ht.at[hblock(y), lanes(ch)]
        return remote(rows_of, rows_of, s_h.at[ch, k], r_h.at[ch, k], at_y(k))

    def first_product(ch):
        for i in range(chunks[ch][0], sum(chunks[ch])):
            cols = slice(i * LANES, (i + 1) * LANES)
            p = dot(wt[...], xt[:, cols])
            part_f[:, cols] = p
            part_b[:, cols] = p.astype(BF16)
        for k in y_order:
            share_of(ch, k).start()

    def add_shares(ch):
        total = part_f[hblock(y), lanes(ch)]
        for k in reversed(y_order):
            share_of(ch, k).wait_recv()
            total = total + got_b[k, :, lanes(ch)].astype(F32)
        share[:, lanes(ch)] = total
        swap(ch).start()

    def activate(ch):
        swap(ch).wait_recv()
        mine, theirs = share[:, lanes(ch)], other[:, lanes(ch)]
        pre = jnp.where(first, mine, theirs)
        cdf = 0.5 * (1.0 + lax.erf(pre * (1.0 / math.sqrt(2.0))))
        dens = jnp.exp(-0.5 * pre * pre) * (1.0 / math.sqrt(2.0 * math.pi))
        made = jnp.where(first, theirs * (cdf + pre * dens), pre * cdf)
        ht[hblock(y), lanes(ch)] = made.astype(BF16)
        for k in y_order:
            spread(ch, k).start()

    def gathered(ch):
        for k in reversed(y_order):
            landing = ht.at[hblock(lax.rem(y + ny - k, ny)), lanes(ch)]
            remote(landing, landing, s_h.at[ch, k], r_h.at[ch, k], at_y(1)).wait_recv()

    def arrived(i):
        for k in range(1, nx):
            landing = block(i, place[(nx - k) % nx])
            remote(landing, landing, s_ax.at[k, i], r_ax.at[k, i], at_x(1)).wait_recv()

    first_product(0)
    add_shares(0)
    activate(0)
    loop(nz, arrived)
    first_product(1)
    first_product(2)
    add_shares(1)
    activate(1)
    add_shares(2)
    activate(2)

    def to_x(k, d):
        at = place[k] * LANES
        return remote(send_c.at[rblock(d), at:at + LANES], got_x.at[k, rblock(d), :],
                      s_cx.at[k, d], r_cx.at[k, d], at_x(k))

    def second_product(ch):
        def one(i):
            d = lax.rem(z + far_first(i), nz)
            send_c[rblock(d), lanes(ch)] = dot(w[rblock(d), :], ht[:, lanes(ch)]).astype(BF16)
            for at in range(chunks[ch][0], sum(chunks[ch])):
                to_x(order[at], d).start()
        loop(nz, one)

    def own_product(i):
        tall = pl.ds(pl.multiple_of(i * 2 * LANES, 2 * LANES), 2 * LANES)
        own_c[tall, :] = dot(w[tall, :], ht[:, :LANES])

    gathered(0)
    loop(width // (2 * LANES), own_product)
    gathered(1)
    second_product(1)
    gathered(2)
    second_product(2)

    step_rows = 2 * LANES

    @pl.when(first)
    def _():
        def grad(i):
            tall = pl.ds(pl.multiple_of(i * step_rows, step_rows), step_rows)
            p = dot(xt[tall, :], ht[...], ((1,), (1,))).astype(BF16)
            o_gu[tall, :] = p[:, :fcols]
            g_give_up[tall, :] = p[:, LANES:]
        loop(width // step_rows, grad)
        remote(g_give_up, g_got_up, s_pair.at[4], r_pair.at[4], partner).start()

    @pl.when(c == 1)
    def _():
        def grad(i):
            tall = pl.ds(pl.multiple_of(i * step_rows, step_rows), step_rows)
            p = dot(ht[...], xt[tall, :], ((1,), (1,))).astype(BF16)
            g_give_dn[:, tall] = p[:LANES, :]
            o_gd[:, tall] = p[LANES:LANES + fcols, :]
        loop(width // step_rows, grad)
        remote(g_give_dn, g_got_dn, s_pair.at[5], r_pair.at[5], partner).start()

    def to_z(k):
        d = lax.rem(z + k, nz)
        return remote(send_z.at[rblock(d), :], got_z.at[z], s_cz.at[k], r_cz.at[z], at_z(k))

    def add_x(d):
        total = own_c[rblock(d), :]
        for k in range(1, nx):
            to_x(k, d).wait_recv()
            total = total + got_x[k, rblock(d), :].astype(F32)
        return total

    def pass_on(i):
        k = far_first(i)
        d = lax.rem(z + k, nz)
        send_z[rblock(d), :] = add_x(d).astype(BF16)
        to_z(k).start()
    loop(nz - 1, pass_on)
    final[:rows, :] = add_x(z)

    def collect(i):
        s = lax.rem(z + far_first(nz - 2 - i), nz)
        remote(got_z.at[s], got_z.at[s], s_cz.at[1], r_cz.at[s], at_z(1)).wait_recv()
        final[:rows, :] += got_z[s].astype(F32)
    loop(nz - 1, collect)

    out_give[...] = jnp.zeros_like(out_give)
    out_give[:half, :] = final[pl.ds(pl.multiple_of((1 - c) * half, 8), half), :].astype(BF16)
    back = remote(out_give, out_got, s_pair.at[6], r_pair.at[6], partner)
    back.start()
    kept = final[pl.ds(pl.multiple_of(c * half, 8), half), :].astype(BF16)

    @pl.when(first)
    def _():
        remote(g_give_dn, g_got_dn, s_pair.at[4], r_pair.at[5], partner).wait_recv()
        o_gd[...] = g_got_dn[:fcols, :]
        o_gt[...] = kept
        back.wait_recv()
        o_out[...] = out_got[:half, :]
        remote(give_dn, wt.at[:LANES, :], s_pair.at[1], r_pair.at[1], partner).wait_send()
        remote(g_give_up, g_got_up, s_pair.at[4], r_pair.at[4], partner).wait_send()

    @pl.when(c == 1)
    def _():
        remote(g_give_up, g_got_up, s_pair.at[5], r_pair.at[4], partner).wait_recv()
        o_gu[...] = g_got_up[:, :fcols]
        o_out[...] = kept
        back.wait_recv()
        o_gt[...] = out_got[:half, :]
        remote(give_up, w.at[:, LANES:], s_pair.at[2], r_pair.at[2], partner).wait_send()
        remote(g_give_dn, g_got_dn, s_pair.at[5], r_pair.at[5], partner).wait_send()

    to_pair.wait_send()
    back.wait_send()
    for ch in range(len(chunks)):
        swap(ch).wait_send()
        for k in y_order:
            share_of(ch, k).wait_send()
            spread(ch, k).wait_send()
    for q in range(4):
        if q < 3:
            over_far(q).wait_send()
        for j in range(3):
            over_near(q, j).wait_send()
    loop(nz - 1, lambda i: to_z(far_first(i)).wait_send())

    def sent(i):
        for k in range(1, nx):
            over_x(k, i).wait_send()
            to_x(k, i).wait_send()
    loop(nz, sent)


def local(shape, tokens, w_up, w_down, out_grad):
    tokens, out_grad = tokens.T, out_grad.T
    nx, ny, nz = shape["gy"], shape["gx"], shape["gz"] // 2
    half = tokens.shape[0]
    rows, padded = 2 * half, -(-half // 16) * 16
    width, fcols = w_up.shape
    count = tokens.shape[1] * nx
    hid = 2 * LANES
    vmem, dma = pltpu.VMEM, pltpu.SemaphoreType.DMA
    scratch = [
        vmem((padded, LANES), BF16), vmem((padded, LANES), BF16), vmem((rows, LANES), F32),
        vmem((width, count), BF16), vmem((width, hid), BF16), vmem((hid, width), BF16),
        vmem((width, LANES), BF16), vmem((LANES, width), BF16),
        vmem((hid, count), F32), vmem((hid, count), BF16), vmem((ny, hid // ny, count), BF16),
        vmem((hid // ny, count), F32), vmem((hid // ny, count), F32), vmem((hid, count), BF16),
        vmem((width, count), BF16), vmem((nx, width, LANES), BF16), vmem((width, LANES), F32),
        vmem((width, LANES), BF16), vmem((nz, rows, LANES), BF16), vmem((rows, LANES), F32),
        vmem((padded, LANES), BF16), vmem((padded, LANES), BF16),
        vmem((width, LANES), BF16), vmem((LANES, width), BF16),
        vmem((width, LANES), BF16), vmem((LANES, width), BF16),
        dma((7,)), dma((7,)), dma((3,)), dma((3,)), dma((4, 3)), dma((4, 3)),
        dma((nx, nz)), dma((nx, nz)),
        dma((3,)), dma((3,)), dma((3, ny)), dma((3, ny)), dma((3, ny)), dma((3, ny)),
        dma((nx, nz)), dma((nx, nz)), dma((nz,)), dma((nz,)),
    ]
    whole = pl.BlockSpec(memory_space=pltpu.VMEM)
    out, grad_tokens, grad_up, grad_down = pl.pallas_call(
        functools.partial(kernel, (nx, ny, nz, rows, half, fcols)),
        out_shape=(
            jax.ShapeDtypeStruct(tokens.shape, BF16), jax.ShapeDtypeStruct(tokens.shape, BF16),
            jax.ShapeDtypeStruct(w_up.shape, BF16), jax.ShapeDtypeStruct(w_down.shape, BF16)),
        in_specs=[whole] * 4,
        out_specs=(whole,) * 4,
        scratch_shapes=scratch,
        compiler_params=pltpu.CompilerParams(
            collective_id=0, has_side_effects=True, vmem_limit_bytes=48 * 1024 * 1024),
    )(tokens, out_grad, w_up, w_down)
    return out.T, grad_tokens.T, grad_up, grad_down


def solution(mesh):
    tokens, up, down = P("gy", ("gx", "gz")), P("gx", ("gz", "gy")), P(("gz", "gy"), "gx")
    return jax.shard_map(
        functools.partial(local, dict(mesh.shape)),
        mesh=mesh,
        in_specs=(tokens, up, down, tokens),
        out_specs=(tokens, tokens, up, down),
        check_vma=False,
    )
```

```python
import functools
import math

import jax
import jax.numpy as jnp
from jax import lax
from jax.experimental import pallas as pl
from jax.experimental.pallas import tpu as pltpu
from jax.sharding import PartitionSpec as P

MESH = pl.DeviceIdType.MESH
BF16, F32 = jnp.bfloat16, jnp.float32
LANES = 128


def dot(left, right, dims=((1,), (0,))):
    return lax.dot_general(left, right, (dims, ((), ())), preferred_element_type=F32)


def kernel(sizes, *refs):
    nx, ny, nz, rows, half, fcols = sizes
    (tok, cot, up_hbm, w_dn, o_out, o_gt, o_gu, o_gd,
     w_up, give, pair_in, own_f, xt, w, wt, give_up, give_dn,
     part_f, part_b, got_b, share, other, ht,
     send_c, got_x, own_c, send_z, got_near, got_far, final, out_give, out_got,
     g_give_up, g_give_dn, g_got_up, g_got_dn,
     s_in, s_pair, r_pair, s_far, r_far, s_near, r_near, s_ax, r_ax, s_swap, r_swap, s_b, r_b, s_h, r_h, s_cx, r_cx, s_cn, r_cn, s_cf, r_cf) = refs
    y, x = lax.axis_index("gx"), lax.axis_index("gy")
    g = lax.axis_index("gz")
    z, c = lax.div(g, 2), lax.rem(g, 2)
    width = xt.shape[0]
    tokens = xt.shape[1]
    hid = ht.shape[0]
    hrows = hid // ny

    def dev(yy, xx, zz, cc):
        return (yy, xx, zz * 2 + cc)

    partner = dev(y, x, z, 1 - c)

    def at_x(k):
        return dev(y, lax.rem(x + k, nx), z, c)

    def at_y(k):
        return dev(lax.rem(y + k, ny), x, z, c)

    def at_z(k):
        return dev(y, x, lax.rem(z + k, nz), c)

    def remote(src, dst, ssem, rsem, device):
        return pltpu.make_async_remote_copy(
            src_ref=src, dst_ref=dst, send_sem=ssem, recv_sem=rsem, device_id=device, device_id_type=MESH)

    def loop(n, body):
        def step(i, carry):
            body(i)
            return carry
        lax.fori_loop(0, n, step, 0)

    def rblock(i):
        return pl.ds(pl.multiple_of(i * rows, 16), rows)

    load = pltpu.make_async_copy(up_hbm, w_up, s_in.at[0])
    load.start()

    barrier = pltpu.get_barrier_semaphore()

    def hello(device):
        pl.semaphore_signal(barrier, inc=1, device_id=device, device_id_type=MESH)

    z_peers = (nz // 2, nz // 4, 3 * nz // 4, 2, nz - 2, 1, nz - 1)
    for k in z_peers:
        hello(at_z(k))
    for k in range(1, ny):
        hello(at_y(k))
    for k in range(1, nx):
        hello(at_x(k))
    hello(partner)

    first = c == 0
    give_dn[...] = jnp.zeros_like(give_dn)
    give_up[...] = jnp.zeros_like(give_up)
    give[...] = jnp.zeros_like(give)
    give[:half, :] = jnp.where(first, cot[...], tok[...])
    own_f[pl.ds(pl.multiple_of(c * half, 8), half), :] = jnp.where(first, tok[...], cot[...]).astype(F32)

    order = (0, 2, 1, 3)
    place = {k: at for at, k in enumerate(order)}
    to_pair = remote(give, pair_in, s_pair.at[0], r_pair.at[0], partner)
    far = (nz // 2, nz // 4, 3 * nz // 4, 0)
    near = (2 + (nz - 4) * c, 1 + (nz - 2) * c, nz - 1 - (nz - 2) * c)

    def back_by(k):
        return lax.rem(z + 2 * nz - k, nz)

    def block(zz, at=0):
        return xt.at[rblock(zz), at * LANES:(at + 1) * LANES]

    def over_far(q):
        return remote(block(z), block(z), s_far.at[q], r_far.at[q], at_z(far[q]))

    def over_near(q, j):
        zz = back_by(far[q])
        return remote(block(zz), block(zz), s_near.at[q, j], r_near.at[q, j], at_z(near[j]))

    def over_x(k, zz):
        return remote(block(zz), block(zz, place[(nx - k) % nx]), s_ax.at[k, zz], r_ax.at[k, zz], at_x(k))

    def send_over_x(zz):
        for k in (2, 1, 3):
            over_x(k, zz).start()

    pl.semaphore_wait(barrier, 1 + len(z_peers) + (nx - 1) + (ny - 1))
    to_pair.start()
    to_pair.wait_recv()
    own_f[pl.ds(pl.multiple_of((1 - c) * half, 8), half), :] = pair_in[:half, :].astype(F32)
    xt[rblock(z), :LANES] = own_f[...].astype(BF16)
    for q in range(3):
        over_far(q).start()
    for j in range(3):
        over_near(3, j).start()
    send_over_x(z)

    load.wait()
    give_dn[:fcols, :] = w_dn[...]
    give_up[:, :fcols] = w_up[...]

    @pl.when(first)
    def _():
        remote(give_dn, wt.at[:LANES, :], s_pair.at[1], r_pair.at[1], partner).start()

    @pl.when(c == 1)
    def _():
        remote(give_up, w.at[:, LANES:], s_pair.at[2], r_pair.at[2], partner).start()

    def take_near(q, j):
        zz = back_by(far[q] + near[j])
        remote(block(zz), block(zz), s_near.at[q, j], r_near.at[q, j], at_z(1)).wait_recv()
        send_over_x(zz)

    @pl.when(first)
    def _():
        w[:, :LANES] = give_up[...]
        remote(give_up, w.at[:, LANES:], s_pair.at[1], r_pair.at[2], partner).wait_recv()

        def turn(i):
            tall = pl.ds(pl.multiple_of(i * LANES, LANES), LANES)
            wt[:, tall] = w[tall, :].T
        loop(width // LANES, turn)

    @pl.when(c == 1)
    def _():
        wt[LANES:, :] = give_dn[...]
        remote(give_dn, wt.at[:LANES, :], s_pair.at[2], r_pair.at[1], partner).wait_recv()

        def turn(i):
            tall = pl.ds(pl.multiple_of(i * LANES, LANES), LANES)
            w[tall, :] = wt[:, tall].T
        loop(width // LANES, turn)

    take_near(3, 1)
    take_near(3, 2)
    for q in (1, 2, 0):
        zz = back_by(far[q])
        remote(block(zz), block(zz), s_far.at[q], r_far.at[q], at_z(1)).wait_recv()
        for j in range(3):
            over_near(q, j).start()
        send_over_x(zz)
    take_near(3, 0)
    for q in (1, 2, 0):
        for j in (1, 2, 0):
            take_near(q, j)

    chunks = ((0, 1), (1, 2), (3, 1))

    def lanes(ch):
        return pl.ds(chunks[ch][0] * LANES, chunks[ch][1] * LANES)

    def hblock(i):
        return pl.ds(pl.multiple_of(i * hrows, 16), hrows)

    y_order = sorted(range(1, ny), key=lambda k: -min(k, ny - k))

    def share_of(ch, k):
        return remote(part_b.at[hblock(lax.rem(y + k, ny)), lanes(ch)], got_b.at[k, :, lanes(ch)],
                      s_b.at[ch, k], r_b.at[ch, k], at_y(k))

    def swap(ch):
        return remote(share.at[:, lanes(ch)], other.at[:, lanes(ch)], s_swap.at[ch], r_swap.at[ch], partner)

    def spread(ch, k):
        rows_of = ht.at[hblock(y), lanes(ch)]
        return remote(rows_of, rows_of, s_h.at[ch, k], r_h.at[ch, k], at_y(k))

    def first_product(ch):
        for i in range(chunks[ch][0], sum(chunks[ch])):
            cols = slice(i * LANES, (i + 1) * LANES)
            p = dot(wt[...], xt[:, cols])
            part_f[:, cols] = p
            part_b[:, cols] = p.astype(BF16)
        for k in y_order:
            share_of(ch, k).start()

    def add_shares(ch):
        total = part_f[hblock(y), lanes(ch)]
        for k in reversed(y_order):
            share_of(ch, k).wait_recv()
            total = total + got_b[k, :, lanes(ch)].astype(F32)
        share[:, lanes(ch)] = total
        swap(ch).start()

    def activate(ch):
        swap(ch).wait_recv()
        mine, theirs = share[:, lanes(ch)], other[:, lanes(ch)]
        pre = jnp.where(first, mine, theirs)
        cdf = 0.5 * (1.0 + lax.erf(pre * (1.0 / math.sqrt(2.0))))
        dens = jnp.exp(-0.5 * pre * pre) * (1.0 / math.sqrt(2.0 * math.pi))
        made = jnp.where(first, theirs * (cdf + pre * dens), pre * cdf)
        ht[hblock(y), lanes(ch)] = made.astype(BF16)
        for k in y_order:
            spread(ch, k).start()

    def gathered(ch):
        for k in reversed(y_order):
            landing = ht.at[hblock(lax.rem(y + ny - k, ny)), lanes(ch)]
            remote(landing, landing, s_h.at[ch, k], r_h.at[ch, k], at_y(1)).wait_recv()

    def arrived(i):
        for k in range(1, nx):
            landing = block(i, place[(nx - k) % nx])
            remote(landing, landing, s_ax.at[k, i], r_ax.at[k, i], at_x(1)).wait_recv()

    first_product(0)
    add_shares(0)
    activate(0)
    loop(nz, arrived)
    first_product(1)
    first_product(2)
    add_shares(1)
    activate(1)
    add_shares(2)
    activate(2)

    hops = near + (0,)
    group = len(hops) * rows

    def slot(q, n):
        return pl.ds((q * len(hops) + n) * rows, rows)

    def goal(q, n):
        return lax.rem(z + far[q] + hops[n], nz)

    def to_x(k, q):
        at, tall = place[k] * LANES, pl.ds(q * group, group)
        return remote(send_c.at[tall, at:at + LANES], got_x.at[k, tall, :], s_cx.at[k, q], r_cx.at[k, q], at_x(k))

    def second_product(ch):
        for q in range(4):
            for n in range(4):
                send_c[slot(q, n), lanes(ch)] = dot(w[rblock(goal(q, n)), :], ht[:, lanes(ch)]).astype(BF16)
            for at in range(chunks[ch][0], sum(chunks[ch])):
                to_x(order[at], q).start()

    gathered(0)
    for q in range(4):
        for n in range(4):
            own_c[slot(q, n), :] = dot(w[rblock(goal(q, n)), :], ht[:, :LANES])
    gathered(1)
    second_product(1)
    gathered(2)
    second_product(2)

    step_rows = 2 * LANES

    @pl.when(first)
    def _():
        def grad(i):
            tall = pl.ds(pl.multiple_of(i * step_rows, step_rows), step_rows)
            p = dot(xt[tall, :], ht[...], ((1,), (1,))).astype(BF16)
            o_gu[tall, :] = p[:, :fcols]
            g_give_up[tall, :] = p[:, LANES:]
        loop(width // step_rows, grad)
        remote(g_give_up, g_got_up, s_pair.at[4], r_pair.at[4], partner).start()

    @pl.when(c == 1)
    def _():
        def grad(i):
            tall = pl.ds(pl.multiple_of(i * step_rows, step_rows), step_rows)
            p = dot(ht[...], xt[tall, :], ((1,), (1,))).astype(BF16)
            g_give_dn[:, tall] = p[:LANES, :]
            o_gd[:, tall] = p[LANES:LANES + fcols, :]
        loop(width // step_rows, grad)
        remote(g_give_dn, g_got_dn, s_pair.at[5], r_pair.at[5], partner).start()

    def to_near(q, n):
        return remote(send_z.at[slot(q, n), :], got_near.at[q, n], s_cn.at[q, n], r_cn.at[q, n], at_z(hops[n]))

    def to_far(q):
        return remote(send_z.at[slot(q, 3), :], got_far.at[q], s_cf.at[q], r_cf.at[q], at_z(far[q]))

    def add_x(q):
        for k in range(1, nx):
            to_x(k, q).wait_recv()
        for n in range(4):
            total = own_c[slot(q, n), :]
            for k in range(1, nx):
                total = total + got_x[k, slot(q, n), :].astype(F32)
            if n < 3:
                send_z[slot(q, n), :] = total.astype(BF16)
                to_near(q, n).start()
            else:
                own_c[slot(q, n), :] = total

    def add_near(q):
        total = own_c[slot(q, 3), :]
        for n in range(3):
            to_near(q, n).wait_recv()
            total = total + got_near[q, n].astype(F32)
        if q < 3:
            send_z[slot(q, 3), :] = total.astype(BF16)
            to_far(q).start()
        return total

    add_x(0)
    add_x(1)
    add_near(0)
    add_x(2)
    add_near(1)
    add_x(3)
    add_near(2)
    total = add_near(3)
    for q in (1, 2, 0):
        to_far(q).wait_recv()
        total = total + got_far[q].astype(F32)
    final[...] = total

    out_give[...] = jnp.zeros_like(out_give)
    out_give[:half, :] = final[pl.ds(pl.multiple_of((1 - c) * half, 8), half), :].astype(BF16)
    back = remote(out_give, out_got, s_pair.at[6], r_pair.at[6], partner)
    back.start()
    kept = final[pl.ds(pl.multiple_of(c * half, 8), half), :].astype(BF16)

    @pl.when(first)
    def _():
        remote(g_give_dn, g_got_dn, s_pair.at[4], r_pair.at[5], partner).wait_recv()
        o_gd[...] = g_got_dn[:fcols, :]
        o_gt[...] = kept
        back.wait_recv()
        o_out[...] = out_got[:half, :]
        remote(give_dn, wt.at[:LANES, :], s_pair.at[1], r_pair.at[1], partner).wait_send()
        remote(g_give_up, g_got_up, s_pair.at[4], r_pair.at[4], partner).wait_send()

    @pl.when(c == 1)
    def _():
        remote(g_give_up, g_got_up, s_pair.at[5], r_pair.at[4], partner).wait_recv()
        o_gu[...] = g_got_up[:, :fcols]
        o_out[...] = kept
        back.wait_recv()
        o_gt[...] = out_got[:half, :]
        remote(give_up, w.at[:, LANES:], s_pair.at[2], r_pair.at[2], partner).wait_send()
        remote(g_give_dn, g_got_dn, s_pair.at[5], r_pair.at[5], partner).wait_send()

    to_pair.wait_send()
    back.wait_send()
    for ch in range(len(chunks)):
        swap(ch).wait_send()
        for k in y_order:
            share_of(ch, k).wait_send()
            spread(ch, k).wait_send()
    for q in range(4):
        if q < 3:
            over_far(q).wait_send()
        for j in range(3):
            over_near(q, j).wait_send()
    for q in range(4):
        if q < 3:
            to_far(q).wait_send()
        for n in range(3):
            to_near(q, n).wait_send()
        for k in range(1, nx):
            to_x(k, q).wait_send()

    def sent(i):
        for k in range(1, nx):
            over_x(k, i).wait_send()
    loop(nz, sent)


def local(shape, tokens, w_up, w_down, out_grad):
    tokens, out_grad = tokens.T, out_grad.T
    nx, ny, nz = shape["gy"], shape["gx"], shape["gz"] // 2
    half = tokens.shape[0]
    rows, padded = 2 * half, -(-half // 16) * 16
    width, fcols = w_up.shape
    count = tokens.shape[1] * nx
    hid = 2 * LANES
    vmem, dma = pltpu.VMEM, pltpu.SemaphoreType.DMA
    scratch = [
        vmem(w_up.shape, BF16),
        vmem((padded, LANES), BF16), vmem((padded, LANES), BF16), vmem((rows, LANES), F32),
        vmem((width, count), BF16), vmem((width, hid), BF16), vmem((hid, width), BF16),
        vmem((width, LANES), BF16), vmem((LANES, width), BF16),
        vmem((hid, count), F32), vmem((hid, count), BF16), vmem((ny, hid // ny, count), BF16),
        vmem((hid // ny, count), F32), vmem((hid // ny, count), F32), vmem((hid, count), BF16),
        vmem((width, count), BF16), vmem((nx, width, LANES), BF16), vmem((width, LANES), F32),
        vmem((width, LANES), BF16), vmem((4, 3, rows, LANES), BF16), vmem((3, rows, LANES), BF16), vmem((rows, LANES), F32),
        vmem((padded, LANES), BF16), vmem((padded, LANES), BF16),
        vmem((width, LANES), BF16), vmem((LANES, width), BF16),
        vmem((width, LANES), BF16), vmem((LANES, width), BF16),
        dma((1,)), dma((7,)), dma((7,)), dma((3,)), dma((3,)), dma((4, 3)), dma((4, 3)),
        dma((nx, nz)), dma((nx, nz)),
        dma((3,)), dma((3,)), dma((3, ny)), dma((3, ny)), dma((3, ny)), dma((3, ny)),
        dma((nx, 4)), dma((nx, 4)), dma((4, 3)), dma((4, 3)), dma((3,)), dma((3,)),
    ]
    whole = pl.BlockSpec(memory_space=pltpu.VMEM)
    out, grad_tokens, grad_up, grad_down = pl.pallas_call(
        functools.partial(kernel, (nx, ny, nz, rows, half, fcols)),
        out_shape=(
            jax.ShapeDtypeStruct(tokens.shape, BF16), jax.ShapeDtypeStruct(tokens.shape, BF16),
            jax.ShapeDtypeStruct(w_up.shape, BF16), jax.ShapeDtypeStruct(w_down.shape, BF16)),
        in_specs=[whole, whole, pl.BlockSpec(memory_space=pltpu.HBM), whole],
        out_specs=(whole,) * 4,
        scratch_shapes=scratch,
        compiler_params=pltpu.CompilerParams(
            collective_id=0, has_side_effects=True, vmem_limit_bytes=48 * 1024 * 1024),
    )(tokens, out_grad, w_up, w_down)
    return out.T, grad_tokens.T, grad_up, grad_down


def solution(mesh):
    tokens, up, down = P("gy", ("gx", "gz")), P("gx", ("gz", "gy")), P(("gz", "gy"), "gx")
    return jax.shard_map(
        functools.partial(local, dict(mesh.shape)),
        mesh=mesh,
        in_specs=(tokens, up, down, tokens),
        out_specs=(tokens, tokens, up, down),
        check_vma=False,
    )
```

```python
import functools
import math

import jax
import jax.numpy as jnp
from jax import lax
from jax.experimental import pallas as pl
from jax.experimental.pallas import tpu as pltpu
from jax.sharding import PartitionSpec as P

MESH = pl.DeviceIdType.MESH
BF16, F32 = jnp.bfloat16, jnp.float32
LANES = 128


def dot(left, right, dims=((1,), (0,))):
    return lax.dot_general(left, right, (dims, ((), ())), preferred_element_type=F32)


def kernel(sizes, *refs):
    nx, ny, nz, rows, half, fcols = sizes
    (tok, cot, up_hbm, w_dn, o_out, o_gt, o_gu, o_gd,
     w_up, give, pair_in, own_f, xt, w, wt, give_up, give_dn,
     part_f, part_b, got_b, share, other, ht,
     send_c, got_x, own_c, send_z, got_near, got_far, final, out_give, out_got,
     g_give_up, g_give_dn, g_got_up, g_got_dn,
     s_in, s_pair, r_pair, s_far, r_far, s_near, r_near, s_ax, r_ax, s_swap, r_swap, s_b, r_b, s_h, r_h, s_cx, r_cx, s_cn, r_cn, s_cf, r_cf) = refs
    y, x = lax.axis_index("gx"), lax.axis_index("gy")
    g = lax.axis_index("gz")
    z, c = lax.div(g, 2), lax.rem(g, 2)
    width = xt.shape[0]
    tokens = xt.shape[1]
    hid = ht.shape[0]
    hrows = hid // ny

    def dev(yy, xx, zz, cc):
        return (yy, xx, zz * 2 + cc)

    partner = dev(y, x, z, 1 - c)

    def at_x(k):
        return dev(y, lax.rem(x + k, nx), z, c)

    def at_y(k):
        return dev(lax.rem(y + k, ny), x, z, c)

    def at_z(k):
        return dev(y, x, lax.rem(z + k, nz), c)

    def remote(src, dst, ssem, rsem, device):
        return pltpu.make_async_remote_copy(
            src_ref=src, dst_ref=dst, send_sem=ssem, recv_sem=rsem, device_id=device, device_id_type=MESH)

    def loop(n, body):
        def step(i, carry):
            body(i)
            return carry
        lax.fori_loop(0, n, step, 0)

    def rblock(i):
        return pl.ds(pl.multiple_of(i * rows, 16), rows)

    load = pltpu.make_async_copy(up_hbm, w_up, s_in.at[0])
    load.start()

    barrier = pltpu.get_barrier_semaphore()

    def hello(device):
        pl.semaphore_signal(barrier, inc=1, device_id=device, device_id_type=MESH)

    z_peers = (nz // 2, nz // 4, 3 * nz // 4, 2, nz - 2, 1, nz - 1)
    for k in z_peers:
        hello(at_z(k))
    for k in range(1, ny):
        hello(at_y(k))
    for k in range(1, nx):
        hello(at_x(k))
    hello(partner)

    first = c == 0
    give_dn[...] = jnp.zeros_like(give_dn)
    give_up[...] = jnp.zeros_like(give_up)
    give[...] = jnp.zeros_like(give)
    give[:half, :] = jnp.where(first, cot[...], tok[...])
    own_f[pl.ds(pl.multiple_of(c * half, 8), half), :] = jnp.where(first, tok[...], cot[...]).astype(F32)

    order = (0, 2, 1, 3)
    place = {k: at for at, k in enumerate(order)}
    to_pair = remote(give, pair_in, s_pair.at[0], r_pair.at[0], partner)
    far = (nz // 2, nz // 4, 3 * nz // 4, 0)
    near = (2 + (nz - 4) * c, 1 + (nz - 2) * c, nz - 1 - (nz - 2) * c)

    def back_by(k):
        return lax.rem(z + 2 * nz - k, nz)

    def block(zz, at=0):
        return xt.at[rblock(zz), at * LANES:(at + 1) * LANES]

    def over_far(q):
        return remote(block(z), block(z), s_far.at[q], r_far.at[q], at_z(far[q]))

    def over_near(q, j):
        zz = back_by(far[q])
        return remote(block(zz), block(zz), s_near.at[q, j], r_near.at[q, j], at_z(near[j]))

    def over_x(k, zz):
        return remote(block(zz), block(zz, place[(nx - k) % nx]), s_ax.at[k, zz], r_ax.at[k, zz], at_x(k))

    def send_over_x(zz):
        for k in (2, 1, 3):
            over_x(k, zz).start()

    pl.semaphore_wait(barrier, 1 + len(z_peers) + (nx - 1) + (ny - 1))
    to_pair.start()
    to_pair.wait_recv()
    own_f[pl.ds(pl.multiple_of((1 - c) * half, 8), half), :] = pair_in[:half, :].astype(F32)
    xt[rblock(z), :LANES] = own_f[...].astype(BF16)
    for q in range(3):
        over_far(q).start()
    for j in range(3):
        over_near(3, j).start()
    send_over_x(z)

    load.wait()
    give_dn[:fcols, :] = w_dn[...]
    give_up[:, :fcols] = w_up[...]

    @pl.when(first)
    def _():
        remote(give_dn, wt.at[:LANES, :], s_pair.at[1], r_pair.at[1], partner).start()

    @pl.when(c == 1)
    def _():
        remote(give_up, w.at[:, LANES:], s_pair.at[2], r_pair.at[2], partner).start()

    def take_near(q, j):
        zz = back_by(far[q] + near[j])
        remote(block(zz), block(zz), s_near.at[q, j], r_near.at[q, j], at_z(1)).wait_recv()
        send_over_x(zz)

    @pl.when(first)
    def _():
        w[:, :LANES] = give_up[...]
        remote(give_up, w.at[:, LANES:], s_pair.at[1], r_pair.at[2], partner).wait_recv()

        def turn(i):
            tall = pl.ds(pl.multiple_of(i * LANES, LANES), LANES)
            wt[:, tall] = w[tall, :].T
        loop(width // LANES, turn)

    @pl.when(c == 1)
    def _():
        wt[LANES:, :] = give_dn[...]
        remote(give_dn, wt.at[:LANES, :], s_pair.at[2], r_pair.at[1], partner).wait_recv()

        def turn(i):
            tall = pl.ds(pl.multiple_of(i * LANES, LANES), LANES)
            w[tall, :] = wt[:, tall].T
        loop(width // LANES, turn)

    take_near(3, 1)
    take_near(3, 2)
    for q in (1, 2, 0):
        zz = back_by(far[q])
        remote(block(zz), block(zz), s_far.at[q], r_far.at[q], at_z(1)).wait_recv()
        for j in range(3):
            over_near(q, j).start()
        send_over_x(zz)
    take_near(3, 0)
    for q in (1, 2, 0):
        for j in (1, 2, 0):
            take_near(q, j)

    chunks = ((0, 1), (1, 2), (3, 1))

    def lanes(ch):
        return pl.ds(chunks[ch][0] * LANES, chunks[ch][1] * LANES)

    def hblock(i):
        return pl.ds(pl.multiple_of(i * hrows, 16), hrows)

    y_order = sorted(range(1, ny), key=lambda k: -min(k, ny - k))

    def share_of(ch, k):
        return remote(part_b.at[hblock(lax.rem(y + k, ny)), lanes(ch)], got_b.at[k, :, lanes(ch)],
                      s_b.at[ch, k], r_b.at[ch, k], at_y(k))

    def swap(ch):
        return remote(share.at[:, lanes(ch)], other.at[:, lanes(ch)], s_swap.at[ch], r_swap.at[ch], partner)

    def spread(ch, k):
        rows_of = ht.at[hblock(y), lanes(ch)]
        return remote(rows_of, rows_of, s_h.at[ch, k], r_h.at[ch, k], at_y(k))

    def first_product(ch):
        for i in range(chunks[ch][0], sum(chunks[ch])):
            cols = slice(i * LANES, (i + 1) * LANES)
            p = dot(wt[...], xt[:, cols])
            part_f[:, cols] = p
            part_b[:, cols] = p.astype(BF16)
        for k in y_order:
            share_of(ch, k).start()

    def add_shares(ch):
        total = part_f[hblock(y), lanes(ch)]
        for k in reversed(y_order):
            share_of(ch, k).wait_recv()
            total = total + got_b[k, :, lanes(ch)].astype(F32)
        share[:, lanes(ch)] = total
        swap(ch).start()

    def activate(ch):
        swap(ch).wait_recv()
        mine, theirs = share[:, lanes(ch)], other[:, lanes(ch)]
        pre = jnp.where(first, mine, theirs)
        cdf = 0.5 * (1.0 + lax.erf(pre * (1.0 / math.sqrt(2.0))))
        dens = jnp.exp(-0.5 * pre * pre) * (1.0 / math.sqrt(2.0 * math.pi))
        made = jnp.where(first, theirs * (cdf + pre * dens), pre * cdf)
        ht[hblock(y), lanes(ch)] = made.astype(BF16)
        for k in y_order:
            spread(ch, k).start()

    def gathered(ch):
        for k in reversed(y_order):
            landing = ht.at[hblock(lax.rem(y + ny - k, ny)), lanes(ch)]
            remote(landing, landing, s_h.at[ch, k], r_h.at[ch, k], at_y(1)).wait_recv()

    def arrived(i):
        for k in range(1, nx):
            landing = block(i, place[(nx - k) % nx])
            remote(landing, landing, s_ax.at[k, i], r_ax.at[k, i], at_x(1)).wait_recv()

    first_product(0)
    add_shares(0)
    activate(0)
    loop(nz, arrived)
    first_product(1)
    first_product(2)
    add_shares(1)
    activate(1)
    add_shares(2)
    activate(2)

    hops = near + (0,)
    group = len(hops) * rows

    def slot(q, n):
        return pl.ds((q * len(hops) + n) * rows, rows)

    def goal(q, n):
        return lax.rem(z + far[q] + hops[n], nz)

    def to_x(k, q):
        at, tall = place[k] * LANES, pl.ds(q * group, group)
        return remote(send_c.at[tall, at:at + LANES], got_x.at[k, tall, :], s_cx.at[k, q], r_cx.at[k, q], at_x(k))

    def second_product(ch):
        for q in range(4):
            for n in range(4):
                send_c[slot(q, n), lanes(ch)] = dot(w[rblock(goal(q, n)), :], ht[:, lanes(ch)]).astype(BF16)
            for at in range(chunks[ch][0], sum(chunks[ch])):
                to_x(order[at], q).start()

    gathered(0)
    for q in range(4):
        for n in range(4):
            own_c[slot(q, n), :] = dot(w[rblock(goal(q, n)), :], ht[:, :LANES])
    gathered(1)
    second_product(1)
    gathered(2)
    second_product(2)

    def to_near(q, n):
        return remote(send_z.at[slot(q, n), :], got_near.at[q, n], s_cn.at[q, n], r_cn.at[q, n], at_z(hops[n]))

    def to_far(q):
        return remote(send_z.at[slot(q, 3), :], got_far.at[q], s_cf.at[q], r_cf.at[q], at_z(far[q]))

    def add_x(q):
        for k in range(1, nx):
            to_x(k, q).wait_recv()
        for n in range(4):
            total = own_c[slot(q, n), :]
            for k in range(1, nx):
                total = total + got_x[k, slot(q, n), :].astype(F32)
            if n < 3:
                send_z[slot(q, n), :] = total.astype(BF16)
                to_near(q, n).start()
            else:
                own_c[slot(q, n), :] = total

    def add_near(q):
        total = own_c[slot(q, 3), :]
        for n in range(3):
            to_near(q, n).wait_recv()
            total = total + got_near[q, n].astype(F32)
        if q < 3:
            send_z[slot(q, 3), :] = total.astype(BF16)
            to_far(q).start()
        return total

    add_x(0)
    add_x(1)
    add_near(0)
    add_x(2)
    add_near(1)
    add_x(3)
    add_near(2)

    step_rows = 2 * LANES

    @pl.when(first)
    def _():
        def grad(i):
            tall = pl.ds(pl.multiple_of(i * step_rows, step_rows), step_rows)
            p = dot(xt[tall, :], ht[...], ((1,), (1,))).astype(BF16)
            o_gu[tall, :] = p[:, :fcols]
            g_give_up[tall, :] = p[:, LANES:]
        loop(width // step_rows, grad)
        remote(g_give_up, g_got_up, s_pair.at[4], r_pair.at[4], partner).start()

    @pl.when(c == 1)
    def _():
        def grad(i):
            tall = pl.ds(pl.multiple_of(i * step_rows, step_rows), step_rows)
            p = dot(ht[...], xt[tall, :], ((1,), (1,))).astype(BF16)
            g_give_dn[:, tall] = p[:LANES, :]
            o_gd[:, tall] = p[LANES:LANES + fcols, :]
        loop(width // step_rows, grad)
        remote(g_give_dn, g_got_dn, s_pair.at[5], r_pair.at[5], partner).start()

    total = add_near(3)
    for q in (1, 2, 0):
        to_far(q).wait_recv()
        total = total + got_far[q].astype(F32)
    final[...] = total

    out_give[...] = jnp.zeros_like(out_give)
    out_give[:half, :] = final[pl.ds(pl.multiple_of((1 - c) * half, 8), half), :].astype(BF16)
    back = remote(out_give, out_got, s_pair.at[6], r_pair.at[6], partner)
    back.start()
    kept = final[pl.ds(pl.multiple_of(c * half, 8), half), :].astype(BF16)

    @pl.when(first)
    def _():
        remote(g_give_dn, g_got_dn, s_pair.at[4], r_pair.at[5], partner).wait_recv()
        o_gd[...] = g_got_dn[:fcols, :]
        o_gt[...] = kept
        back.wait_recv()
        o_out[...] = out_got[:half, :]
        remote(give_dn, wt.at[:LANES, :], s_pair.at[1], r_pair.at[1], partner).wait_send()
        remote(g_give_up, g_got_up, s_pair.at[4], r_pair.at[4], partner).wait_send()

    @pl.when(c == 1)
    def _():
        remote(g_give_up, g_got_up, s_pair.at[5], r_pair.at[4], partner).wait_recv()
        o_gu[...] = g_got_up[:, :fcols]
        o_out[...] = kept
        back.wait_recv()
        o_gt[...] = out_got[:half, :]
        remote(give_up, w.at[:, LANES:], s_pair.at[2], r_pair.at[2], partner).wait_send()
        remote(g_give_dn, g_got_dn, s_pair.at[5], r_pair.at[5], partner).wait_send()

    to_pair.wait_send()
    back.wait_send()
    for ch in range(len(chunks)):
        swap(ch).wait_send()
        for k in y_order:
            share_of(ch, k).wait_send()
            spread(ch, k).wait_send()
    for q in range(4):
        if q < 3:
            over_far(q).wait_send()
        for j in range(3):
            over_near(q, j).wait_send()
    for q in range(4):
        if q < 3:
            to_far(q).wait_send()
        for n in range(3):
            to_near(q, n).wait_send()
        for k in range(1, nx):
            to_x(k, q).wait_send()

    def sent(i):
        for k in range(1, nx):
            over_x(k, i).wait_send()
    loop(nz, sent)


def local(shape, tokens, w_up, w_down, out_grad):
    tokens, out_grad = tokens.T, out_grad.T
    nx, ny, nz = shape["gy"], shape["gx"], shape["gz"] // 2
    half = tokens.shape[0]
    rows, padded = 2 * half, -(-half // 16) * 16
    width, fcols = w_up.shape
    count = tokens.shape[1] * nx
    hid = 2 * LANES
    vmem, dma = pltpu.VMEM, pltpu.SemaphoreType.DMA
    scratch = [
        vmem(w_up.shape, BF16),
        vmem((padded, LANES), BF16), vmem((padded, LANES), BF16), vmem((rows, LANES), F32),
        vmem((width, count), BF16), vmem((width, hid), BF16), vmem((hid, width), BF16),
        vmem((width, LANES), BF16), vmem((LANES, width), BF16),
        vmem((hid, count), F32), vmem((hid, count), BF16), vmem((ny, hid // ny, count), BF16),
        vmem((hid // ny, count), F32), vmem((hid // ny, count), F32), vmem((hid, count), BF16),
        vmem((width, count), BF16), vmem((nx, width, LANES), BF16), vmem((width, LANES), F32),
        vmem((width, LANES), BF16), vmem((4, 3, rows, LANES), BF16), vmem((3, rows, LANES), BF16), vmem((rows, LANES), F32),
        vmem((padded, LANES), BF16), vmem((padded, LANES), BF16),
        vmem((width, LANES), BF16), vmem((LANES, width), BF16),
        vmem((width, LANES), BF16), vmem((LANES, width), BF16),
        dma((1,)), dma((7,)), dma((7,)), dma((3,)), dma((3,)), dma((4, 3)), dma((4, 3)),
        dma((nx, nz)), dma((nx, nz)),
        dma((3,)), dma((3,)), dma((3, ny)), dma((3, ny)), dma((3, ny)), dma((3, ny)),
        dma((nx, 4)), dma((nx, 4)), dma((4, 3)), dma((4, 3)), dma((3,)), dma((3,)),
    ]
    whole = pl.BlockSpec(memory_space=pltpu.VMEM)
    out, grad_tokens, grad_up, grad_down = pl.pallas_call(
        functools.partial(kernel, (nx, ny, nz, rows, half, fcols)),
        out_shape=(
            jax.ShapeDtypeStruct(tokens.shape, BF16), jax.ShapeDtypeStruct(tokens.shape, BF16),
            jax.ShapeDtypeStruct(w_up.shape, BF16), jax.ShapeDtypeStruct(w_down.shape, BF16)),
        in_specs=[whole, whole, pl.BlockSpec(memory_space=pltpu.HBM), whole],
        out_specs=(whole,) * 4,
        scratch_shapes=scratch,
        compiler_params=pltpu.CompilerParams(
            collective_id=0, has_side_effects=True, vmem_limit_bytes=48 * 1024 * 1024),
    )(tokens, out_grad, w_up, w_down)
    return out.T, grad_tokens.T, grad_up, grad_down


def solution(mesh):
    tokens, up, down = P("gy", ("gx", "gz")), P("gx", ("gz", "gy")), P(("gz", "gy"), "gx")
    return jax.shard_map(
        functools.partial(local, dict(mesh.shape)),
        mesh=mesh,
        in_specs=(tokens, up, down, tokens),
        out_specs=(tokens, tokens, up, down),
        check_vma=False,
    )
```
